32 devices in a mesh: row: 4 (over x, core), col: 8 (over z, y).
Axes of the slice: x: 2, y: 2, z: 4, core: 2. Of those that a mesh axis runs over, the one named last changes fastest.
Arguments:
- a_blocks: float32 [4, 8, 2, 2, 128, 128], P('row', 'col'), may hold values from -0.5 to 0.5
- a_rows: int32 [4, 8, 2, 2], P('row', 'col'), may hold values from 0 to 3, as said below
- b_blocks: float32 [4, 8, 2, 4, 128, 128], P('row', 'col'), may hold values from -6 to 6
- send_list: int32 [4, 8, 2, 4, 2], P('row', 'col'), may hold values from -1 to 3, as said below
- c_partial: float32 [4, 8, 4, 128, 128], P('row', 'col'), may hold values from -6 to 6
- c_list: int32 [4, 8, 4], P('row', 'col'), may hold values from 0 to 7, as said below
Outputs:
- c_blocks: float32 [4, 8, 4, 128, 128], P('row', 'col')
The draws below stay inside these ranges and needn't reach their ends.
Inputs may be any that keep to these rules, and one draw needn't show every extreme that they name: The 2 entries of a_rows for one device and one section are distinct. `send_list`: each list holds 1 to 2 distinct block numbers first, then -1 in the rest of its slots. `c_list`: the 4 entries of a device are distinct.
All inputs are finite; a program needn't handle non-finite values.
Results may differ from the reference program's by a relative error of at most 0.0003.
Values sent between devices are 32-bit elements; how exact they have to be, the bound alone decides.
A program may use at most 64 MiB of HBM per device.

```python
import jax
import jax.numpy as jnp
from jax import lax

BS = 128
SECTIONS = 2
RB = 4
CB = 2
NA = 2
SLOT = 2
NC = 4
NB = 4
N_ROW = 4
N_COL = 8


def draw_a_rows(key, part):
    key = jax.random.fold_in(key, 11)
    total = N_ROW * N_COL * SECTIONS
    keys = jax.random.split(key, total)
    chosen = jax.vmap(lambda one_key: jax.random.permutation(one_key, RB)[:NA])(keys)
    return chosen.astype(jnp.int32).reshape((N_ROW, N_COL, SECTIONS, NA))


def draw_send_list(key, part):
    key = jax.random.fold_in(key, 23)
    total = N_ROW * N_COL * SECTIONS * N_ROW
    key_perm, key_count = jax.random.split(key)
    keys = jax.random.split(key_perm, total)
    chosen = jax.vmap(lambda one_key: jax.random.permutation(one_key, NB)[:SLOT])(keys)
    counts = jax.random.randint(key_count, (total, 1), 1, SLOT + 1)
    position = jnp.arange(SLOT, dtype=jnp.int32)[None, :]
    listed = jnp.where(position < counts, chosen, -1)
    return listed.astype(jnp.int32).reshape((N_ROW, N_COL, SECTIONS, N_ROW, SLOT))


def draw_c_list(key, part):
    key = jax.random.fold_in(key, 37)
    total = N_ROW * N_COL
    keys = jax.random.split(key, total)
    chosen = jax.vmap(lambda one_key: jax.random.permutation(one_key, RB * CB)[:NC])(keys)
    return chosen.astype(jnp.int32).reshape((N_ROW, N_COL, NC))


def steps_of(key, shape, shards, least, high):
    gain = 1.0
    for axis_at, parts in shards:
        heights = jax.random.uniform(jax.random.fold_in(jax.random.fold_in(key, 6), axis_at), (parts,), jnp.float32, least / len(shards), high / len(shards))
        gain = gain * jnp.repeat(jnp.exp(heights), shape[axis_at] // parts).reshape((-1,) + (1,) * (len(shape) - 1 - axis_at))
    return gain


def centred(own_key, shape, width, reach, pieces=(), kind=jnp.bfloat16):
    gain = steps_of(own_key, shape, pieces, -0.22, 0.18) if pieces else 1.0
    values = jax.random.normal(own_key, shape, jnp.float32) * width * gain
    return jnp.minimum(jnp.maximum(values, -reach), reach).astype(kind)


def setup_inputs(seed: int = 0) -> dict:
    key_of = jax.random.split(jax.random.key(seed), 7)
    a_blocks = centred(key_of[0], (N_ROW, N_COL, SECTIONS, NA, BS, BS), BS ** -0.5, 0.5, ((0, 4), (1, 8)), jnp.float32)
    a_rows = draw_a_rows(jax.random.fold_in(key_of[6], 71), 0)
    b_blocks = centred(key_of[2], (N_ROW, N_COL, SECTIONS, NB, BS, BS), 1.0, 6.0, ((0, 4), (1, 8)), jnp.float32)
    send_list = draw_send_list(jax.random.fold_in(key_of[6], 71), 0)
    c_partial = centred(key_of[4], (N_ROW, N_COL, NC, BS, BS), 1.0, 6.0, ((0, 4), (1, 8)), jnp.float32)
    c_list = draw_c_list(jax.random.fold_in(key_of[6], 71), 0)
    return dict(a_blocks=a_blocks, a_rows=a_rows, b_blocks=b_blocks, send_list=send_list, c_partial=c_partial, c_list=c_list)


def device_term(grid_row, grid_col, section_index, a_blocks, a_rows, b_blocks, send_list):
    per_row = N_COL // N_ROW
    entries = send_list[:, grid_col, section_index, grid_row, :]
    filled = entries >= 0
    entry = jnp.maximum(entries, 0)
    source = jnp.arange(N_ROW, dtype=jnp.int32)[:, None]
    blocks = b_blocks[source, grid_col, section_index, entry]
    blocks = jnp.where(filled[:, :, None, None], blocks, jnp.zeros_like(blocks))
    inner = source * per_row + entry // CB
    column = entry % CB
    a_chosen = a_blocks[grid_row, inner, section_index]
    block_rows = a_rows[grid_row, inner, section_index]
    products = jnp.einsum("qtnxy,qtyz->qtnxz", a_chosen, blocks, precision=lax.Precision.HIGHEST)
    target = block_rows * CB + column[:, :, None]
    onehot = (target[..., None] == jnp.arange(RB * CB, dtype=jnp.int32)).astype(jnp.float32)
    return jnp.einsum("qtnc,qtnxz->cxz", onehot, products, precision=lax.Precision.HIGHEST)


def reference(a_blocks, a_rows, b_blocks, send_list, c_partial, c_list):
    def one_device(flat_index):
        grid_row = flat_index // N_COL
        grid_col = flat_index % N_COL
        running = jnp.zeros((RB * CB, BS, BS), jnp.float32)
        for section_index in range(SECTIONS):
            running = running + device_term(grid_row, grid_col, section_index, a_blocks, a_rows, b_blocks, send_list)
        return c_partial[grid_row, grid_col] + running[c_list[grid_row, grid_col]]

    stacked = lax.map(one_device, jnp.arange(N_ROW * N_COL, dtype=jnp.int32))
    return stacked.reshape((N_ROW, N_COL, NC, BS, BS))
```

```python
import functools

import jax
import jax.numpy as jnp
from jax import lax
from jax.experimental import pallas as pl
from jax.experimental.pallas import tpu as pltpu
from jax.sharding import PartitionSpec as P

BS = 128
SECTIONS = 2
NA = 2
SLOT = 2
NC = 4
NB = 4
CB = 2
BLOCKS = SECTIONS * NA
SLOTS = SECTIONS * SLOT
EARLY = 3
MESH = pl.DeviceIdType.MESH


def kernel(R, N, arows, slist, clist, a_ref, b_ref, cp_ref, out_ref,
           abuf, bsrc, stage, bbuf, bhi, blo, mtile, mbuf, msm,
           zsend, zrecv, ysend, yrecv, bsend, brecv, msend, mrecv, lsem):
    L = N // 2
    row = lax.axis_index("row")
    col = lax.axis_index("col")
    z = col // 2
    y = col % 2
    pair = 2 * z + 1 - y

    b_in = pltpu.make_async_copy(b_ref.at[0, 0], bsrc, lsem.at[0])
    a_in = pltpu.make_async_copy(a_ref.at[0, 0], abuf.at[col], lsem.at[1])
    c_in = pltpu.make_async_copy(cp_ref.at[0, 0], out_ref.at[0, 0], lsem.at[2])
    b_in.start()
    a_in.start()
    c_in.start()

    barrier = pltpu.get_barrier_semaphore()
    for o in range(1, N):
        pl.semaphore_signal(barrier, inc=1, device_id=(row, (col + o) % N), device_id_type=MESH)
    for o in range(1, R):
        pl.semaphore_signal(barrier, inc=1, device_id=((row + o) % R, col), device_id_type=MESH)

    lane = lax.broadcasted_iota(jnp.int32, (1, 128), 1)
    tile = jnp.zeros((1, 128), jnp.int32)
    for s in range(SECTIONS):
        for a in range(NA):
            tile = jnp.where(lane == s * NA + a, arows[0, 0, s, a], tile)
        for r in range(R):
            for t in range(SLOT):
                tile = jnp.where(lane == BLOCKS + (s * R + r) * SLOT + t, slist[0, 0, s, r, t], tile)
    mtile[...] = tile
    mbuf[col] = tile
    mbuf[N + row] = tile
    bbuf[R * SLOTS] = jnp.zeros((BS, BS), jnp.float32)

    pl.semaphore_wait(barrier, N - 1 + R - 1)

    def own(k):
        return a_ref.at[0, 0, k // NA, k % NA]

    def held(src, k):
        return abuf.at[src, k // NA, k % NA]

    def line(up, d, ci, first=False):
        begin = z - (d - 1) if up else z + (d - 1)
        src = 2 * begin + (y if ci < BLOCKS else 1 - y)
        k = ci if ci < BLOCKS else EARLY
        way = 0 if up else 1
        return pltpu.make_async_remote_copy(
            src_ref=own(k) if first and ci < BLOCKS else held(src, k),
            dst_ref=held(src, k),
            send_sem=zsend.at[way, d - 1, ci],
            recv_sem=zrecv.at[way, d - 1, ci],
            device_id=(row, col + 2 if up else col - 2),
            device_id_type=MESH,
        )

    def line_sends(up, d):
        return jnp.logical_and(z + 1 < L, z - (d - 1) >= 0) if up else jnp.logical_and(z >= 1, z + (d - 1) < L)

    def line_gets(up, d):
        return z - d >= 0 if up else z + d < L

    def line_got(up, d, ci):
        begin = z - d if up else z + d
        src = 2 * begin + (y if ci < BLOCKS else 1 - y)
        k = ci if ci < BLOCKS else EARLY
        way = 0 if up else 1
        return pltpu.make_async_remote_copy(
            src_ref=held(src, k), dst_ref=held(src, k),
            send_sem=zsend.at[way, d - 1, ci], recv_sem=zrecv.at[way, d - 1, ci],
            device_id=(row, pair), device_id_type=MESH)

    def across(begin, k, first=False):
        src = 2 * begin + y
        return pltpu.make_async_remote_copy(
            src_ref=own(k) if first else held(src, k), dst_ref=held(src, k),
            send_sem=ysend.at[begin, k], recv_sem=yrecv.at[begin, k],
            device_id=(row, pair), device_id_type=MESH)

    def across_got(begin, k):
        src = 2 * begin + 1 - y
        return pltpu.make_async_remote_copy(
            src_ref=held(src, k), dst_ref=held(src, k),
            send_sem=ysend.at[begin, k], recv_sem=yrecv.at[begin, k],
            device_id=(row, pair), device_id_type=MESH)

    order = (EARLY,) + tuple(k for k in range(BLOCKS) if k != EARLY)
    late = tuple(k for k in range(BLOCKS) if k != EARLY)
    for k in order:
        across(z, k, True).start()
        for up in (True, False):
            pl.when(line_sends(up, 1))(lambda up=up, k=k: line(up, 1, k, True).start())

    def tell(o, along_col):
        at = o if along_col else N + o
        to = (row, (col + o) % N) if along_col else ((row + o) % R, col)
        place = col if along_col else N + row
        return pltpu.make_async_remote_copy(
            src_ref=mtile, dst_ref=mbuf.at[place], send_sem=msend.at[at], recv_sem=mrecv.at[at],
            device_id=to, device_id_type=MESH)

    def told(o, along_col):
        at = o if along_col else N + o
        place = (col - o + N) % N if along_col else N + (row - o + R) % R
        return pltpu.make_async_remote_copy(
            src_ref=mtile, dst_ref=mbuf.at[place], send_sem=msend.at[at], recv_sem=mrecv.at[at],
            device_id=(row, pair), device_id_type=MESH)

    peers = [(o, True) for o in range(1, N)] + [(o, False) for o in range(1, R)]
    for peer in peers:
        tell(*peer).start()

    b_in.wait()

    def give(o):
        return pltpu.make_async_remote_copy(
            src_ref=stage.at[o], dst_ref=bbuf.at[pl.ds(row * SLOTS, SLOTS)],
            send_sem=bsend.at[o], recv_sem=brecv.at[o],
            device_id=((row + o) % R, col), device_id_type=MESH)

    def given(o):
        q = (row - o + R) % R
        return pltpu.make_async_remote_copy(
            src_ref=stage.at[o], dst_ref=bbuf.at[pl.ds(q * SLOTS, SLOTS)],
            send_sem=bsend.at[o], recv_sem=brecv.at[o],
            device_id=((row + o) % R, col), device_id_type=MESH)

    for o in sorted(range(R), key=lambda o: (o == 0, abs(o - R // 2))):
        to = (row + o) % R
        for s in range(SECTIONS):
            for t in range(SLOT):
                entry = jnp.maximum(slist[0, 0, s, to, t], 0)
                if o:
                    stage[o, s * SLOT + t] = bsrc[s, entry]
                else:
                    bbuf[row * SLOTS + s * SLOT + t] = bsrc[s, entry]
        if o:
            give(o).start()

    across_got(z, EARLY).wait_recv()
    for up in (True, False):
        pl.when(line_sends(up, 1))(lambda up=up: line(up, 1, BLOCKS).start())

    def step(d, carry):
        for ci in late + (EARLY, BLOCKS):
            for up in (True, False):
                @pl.when(line_gets(up, d))
                def _():
                    line_got(up, d, ci).wait_recv()
                    pl.when(line_sends(up, d + 1))(lambda: line(up, d + 1, ci).start())
                    if ci in late:
                        across(z - d if up else z + d, ci).start()
        return carry

    lax.fori_loop(1, L, step, 0)

    a_in.wait()
    c_in.wait()
    for peer in peers:
        told(*peer).wait_recv()
    to_scalar = pltpu.make_async_copy(mbuf, msm, lsem.at[3])
    to_scalar.start()
    for o in range(1, R):
        given(o).wait_recv()

    def split(at, carry):
        block = bbuf[at]
        high = block.astype(jnp.bfloat16)
        bhi[at] = high
        blo[at] = (block - high.astype(jnp.float32)).astype(jnp.bfloat16)
        return carry

    lax.fori_loop(0, R * SLOTS + 1, split, 0)
    to_scalar.wait()

    for begin in range(L):
        for k in late:
            across_got(begin, k).wait_recv()

    none = R * SLOTS
    wanted_i = [clist[0, 0, m] // CB for m in range(NC)]
    wanted_j = [clist[0, 0, m] % CB for m in range(NC)]

    def multiply(src):
        q = src // 2
        h = src % 2
        for s in range(SECTIONS):
            first = q * SLOTS + s * SLOT
            filled = [msm[N + q, 0, BLOCKS + (s * R + row) * SLOT + t] for t in range(SLOT)]
            at = []
            for j in range(CB):
                entry = h * CB + j
                at.append(jnp.where(filled[0] == entry, first, jnp.where(filled[1] == entry, first + 1, none)))
            rows = [msm[src, 0, s * NA + a] for a in range(NA)]
            left = jnp.concatenate([abuf[src, s, a] for a in range(NA)], axis=1)
            lhi = left.astype(jnp.bfloat16)
            llo = (left - lhi.astype(jnp.float32)).astype(jnp.bfloat16)
            highs, lows = [], []
            for m in range(NC):
                slot = jnp.where(wanted_j[m] == 0, at[0], at[1])
                places = [jnp.where(rows[a] == wanted_i[m], slot, none) for a in range(NA)]
                highs.append(jnp.concatenate([bhi[p] for p in places], axis=0))
                lows.append(jnp.concatenate([blo[p] for p in places], axis=0))
            rhi = jnp.concatenate(highs, axis=1)
            rlo = jnp.concatenate(lows, axis=1)
            total = jnp.dot(lhi, rhi, preferred_element_type=jnp.float32)
            total += jnp.dot(lhi, rlo, preferred_element_type=jnp.float32)
            total += jnp.dot(llo, rhi, preferred_element_type=jnp.float32)
            for m in range(NC):
                out_ref[0, 0, m] += total[:, m * BS:(m + 1) * BS]

    def all_of(src, carry):
        multiply(src)
        return carry

    lax.fori_loop(0, N, all_of, 0)

    for begin in range(L):
        for k in late:
            across(begin, k).wait_send()
    across(z, EARLY).wait_send()

    def drain(d, carry):
        for ci in range(BLOCKS + 1):
            for up in (True, False):
                pl.when(line_sends(up, d))(lambda up=up, ci=ci: line(up, d, ci).wait_send())
        return carry

    lax.fori_loop(1, L, drain, 0)
    for o in range(1, R):
        give(o).wait_send()
    for peer in peers:
        tell(*peer).wait_send()


def body(a_blocks, a_rows, b_blocks, send_list, c_partial, c_list):
    R = lax.axis_size("row")
    N = lax.axis_size("col")
    L = N // 2
    smem = pl.BlockSpec(memory_space=pltpu.SMEM)
    hbm = pl.BlockSpec(memory_space=pl.ANY)
    dma = pltpu.SemaphoreType.DMA
    return pl.pallas_call(
        functools.partial(kernel, R, N),
        out_shape=jax.ShapeDtypeStruct((1, 1, NC, BS, BS), jnp.float32),
        in_specs=[smem, smem, smem, hbm, hbm, hbm],
        out_specs=pl.BlockSpec(memory_space=pltpu.VMEM),
        scratch_shapes=[
            pltpu.VMEM((N, SECTIONS, NA, BS, BS), jnp.float32),
            pltpu.VMEM((SECTIONS, NB, BS, BS), jnp.float32),
            pltpu.VMEM((R, SLOTS, BS, BS), jnp.float32),
            pltpu.VMEM((R * SLOTS + 1, BS, BS), jnp.float32),
            pltpu.VMEM((R * SLOTS + 1, BS, BS), jnp.bfloat16),
            pltpu.VMEM((R * SLOTS + 1, BS, BS), jnp.bfloat16),
            pltpu.VMEM((1, 128), jnp.int32),
            pltpu.VMEM((N + R, 1, 128), jnp.int32),
            pltpu.SMEM((N + R, 1, 128), jnp.int32),
            dma((2, L, BLOCKS + 1)),
            dma((2, L, BLOCKS + 1)),
            dma((L, BLOCKS)),
            dma((L, BLOCKS)),
            dma((R,)),
            dma((R,)),
            dma((N + R,)),
            dma((N + R,)),
            dma((4,)),
        ],
        compiler_params=pltpu.CompilerParams(
            collective_id=0, has_side_effects=True, vmem_limit_bytes=48 * 1024 * 1024
        ),
    )(a_rows, send_list, c_list, a_blocks, b_blocks, c_partial)


def solution(mesh):
    placed = (
        P("row", "col", None, None, None, None),
        P("row", "col", None, None),
        P("row", "col", None, None, None, None),
        P("row", "col", None, None, None),
        P("row", "col", None, None, None),
        P("row", "col", None),
    )
    return jax.shard_map(
        body,
        mesh=mesh,
        in_specs=placed,
        out_specs=P("row", "col", None, None, None),
        check_vma=False,
    )
```

```python
import functools

import jax
import jax.numpy as jnp
from jax import lax
from jax.experimental import pallas as pl
from jax.experimental.pallas import tpu as pltpu
from jax.sharding import PartitionSpec as P

BS = 128
SECTIONS = 2
NA = 2
SLOT = 2
NC = 4
NB = 4
CB = 2
BLOCKS = SECTIONS * NA
SLOTS = SECTIONS * SLOT
ROWS = BLOCKS * BS
CUTS = (0, 88, 192, 296, 400, ROWS)
PIECES = len(CUTS) - 1
EARLY = 0
LISTS = PIECES
LATE = (LISTS,) + tuple(range(1, PIECES))
OTHER = PIECES + 1
LINE = (LISTS, EARLY) + tuple(range(1, PIECES)) + (OTHER,)
MESH = pl.DeviceIdType.MESH


def kernel(R, N, arows, slist, clist, a_ref, b_ref, cp_ref, out_ref,
           abuf, bsrc, stage, bbuf, bhi, blo, mtile, mbuf, msm,
           zsend, zrecv, ysend, yrecv, bsend, brecv, msend, mrecv, msem, lsem):
    L = N // 2
    row = lax.axis_index("row")
    col = lax.axis_index("col")
    z = col // 2
    y = col % 2
    pair = 2 * z + 1 - y

    barrier = pltpu.get_barrier_semaphore()
    pl.when(z + 1 < L)(lambda: pl.semaphore_signal(barrier, inc=1, device_id=(row, col + 2), device_id_type=MESH))
    pl.when(z >= 1)(lambda: pl.semaphore_signal(barrier, inc=1, device_id=(row, col - 2), device_id_type=MESH))
    pl.semaphore_signal(barrier, inc=1, device_id=(row, pair), device_id_type=MESH)
    for o in range(1, R):
        pl.semaphore_signal(barrier, inc=1, device_id=((row + o) % R, col), device_id_type=MESH)

    b_in = pltpu.make_async_copy(b_ref.at[0, 0], bsrc, lsem.at[0])
    a_in = pltpu.make_async_copy(a_ref.at[0, 0], abuf.at[col], lsem.at[1])
    c_in = pltpu.make_async_copy(cp_ref.at[0, 0], out_ref.at[0, 0], lsem.at[2])
    b_in.start()
    a_in.start()
    c_in.start()

    lane = lax.broadcasted_iota(jnp.int32, (1, 128), 1)
    tile = jnp.zeros((1, 128), jnp.int32)
    for s in range(SECTIONS):
        for a in range(NA):
            tile = jnp.where(lane == s * NA + a, arows[0, 0, s, a], tile)
        for r in range(R):
            for t in range(SLOT):
                tile = jnp.where(lane == BLOCKS + (s * R + r) * SLOT + t, slist[0, 0, s, t, r], tile)
    mtile[...] = tile
    mbuf[col] = tile
    mbuf[N + row] = tile

    edge = jnp.where(z + 1 < L, 1, 0) + jnp.where(z >= 1, 1, 0)
    pl.semaphore_wait(barrier, R + edge)

    def own(k):
        return mtile if k == LISTS else a_ref.at[0, 0, pl.ds(CUTS[k], CUTS[k + 1] - CUTS[k])]

    def held(src, k):
        return mbuf.at[src] if k == LISTS else abuf.at[src, pl.ds(CUTS[k], CUTS[k + 1] - CUTS[k])]

    def line_piece(begin, ci):
        return (2 * begin + 1 - y, EARLY) if ci == OTHER else (2 * begin + y, ci)

    def line(up, d, ci, first=False):
        src, k = line_piece(z - (d - 1) if up else z + (d - 1), ci)
        way = 0 if up else 1
        return pltpu.make_async_remote_copy(
            src_ref=own(k) if first and ci != OTHER else held(src, k),
            dst_ref=held(src, k),
            send_sem=zsend.at[way, d - 1, ci],
            recv_sem=zrecv.at[way, d - 1, ci],
            device_id=(row, col + 2 if up else col - 2),
            device_id_type=MESH,
        )

    def line_sends(up, d):
        return jnp.logical_and(z + 1 < L, z - (d - 1) >= 0) if up else jnp.logical_and(z >= 1, z + (d - 1) < L)

    def line_gets(up, d):
        return z - d >= 0 if up else z + d < L

    def line_got(up, d, ci):
        src, k = line_piece(z - d if up else z + d, ci)
        way = 0 if up else 1
        return pltpu.make_async_remote_copy(
            src_ref=held(src, k), dst_ref=held(src, k),
            send_sem=zsend.at[way, d - 1, ci], recv_sem=zrecv.at[way, d - 1, ci],
            device_id=(row, pair), device_id_type=MESH)

    def across(begin, k, first=False):
        src = 2 * begin + y
        return pltpu.make_async_remote_copy(
            src_ref=own(k) if first else held(src, k), dst_ref=held(src, k),
            send_sem=ysend.at[begin, k], recv_sem=yrecv.at[begin, k],
            device_id=(row, pair), device_id_type=MESH)

    def across_got(begin, k):
        src = 2 * begin + 1 - y
        return pltpu.make_async_remote_copy(
            src_ref=held(src, k), dst_ref=held(src, k),
            send_sem=ysend.at[begin, k], recv_sem=yrecv.at[begin, k],
            device_id=(row, pair), device_id_type=MESH)

    for k in LINE:
        if k != OTHER:
            across(z, k, True).start()
            for up in (True, False):
                pl.when(line_sends(up, 1))(lambda up=up, k=k: line(up, 1, k, True).start())

    def tell(o):
        return pltpu.make_async_remote_copy(
            src_ref=mtile, dst_ref=mbuf.at[N + row], send_sem=msend.at[o], recv_sem=mrecv.at[o],
            device_id=((row + o) % R, col), device_id_type=MESH)

    def told(o):
        return pltpu.make_async_remote_copy(
            src_ref=mtile, dst_ref=mbuf.at[N + (row - o + R) % R], send_sem=msend.at[o], recv_sem=mrecv.at[o],
            device_id=(row, pair), device_id_type=MESH)

    for o in range(1, R):
        tell(o).start()

    b_in.wait()

    def give(o, q):
        return pltpu.make_async_remote_copy(
            src_ref=stage.at[o], dst_ref=bbuf.at[pl.ds(q * SLOTS, SLOTS)],
            send_sem=bsend.at[o], recv_sem=brecv.at[o],
            device_id=((row + o) % R, col), device_id_type=MESH)

    for o in sorted(range(R), key=lambda o: (o == 0, abs(o - R // 2))):
        to = (row + o) % R
        for s in range(SECTIONS):
            for t in range(SLOT):
                entry = jnp.maximum(slist[0, 0, s, t, to], 0)
                if o:
                    stage[o, s * SLOT + t] = bsrc[s, entry]
                else:
                    bbuf[row * SLOTS + s * SLOT + t] = bsrc[s, entry]
        if o:
            give(o, row).start()

    across_got(z, EARLY).wait_recv()
    for up in (True, False):
        pl.when(line_sends(up, 1))(lambda up=up: line(up, 1, OTHER).start())

    def step(d, carry):
        for ci in LINE:
            for up in (True, False):
                @pl.when(line_gets(up, d))
                def _():
                    line_got(up, d, ci).wait_recv()
                    pl.when(line_sends(up, d + 1))(lambda: line(up, d + 1, ci).start())
                    if ci in LATE:
                        across(z - d if up else z + d, ci).start()
        return carry

    none = R * SLOTS

    def split(at, carry):
        block = bbuf[at]
        high = block.astype(jnp.bfloat16)
        bhi[at] = high
        blo[at] = (block - high.astype(jnp.float32)).astype(jnp.bfloat16)
        return carry

    def lists_in(src):
        return pltpu.make_async_copy(mbuf.at[src], msm.at[src], msem.at[src])

    def each(least, most, do):
        def one(begin, carry):
            away = jnp.maximum(begin - z, z - begin)
            pl.when(jnp.logical_and(away >= least, away <= most))(lambda: do(begin))
            return carry
        lax.fori_loop(0, L, one, 0)

    def lists_across(begin):
        across_got(begin, LISTS).wait_recv()
        lists_in(2 * begin + 1 - y).start()

    wanted_i = [clist[0, 0, m] // CB for m in range(NC)]
    wanted_j = [clist[0, 0, m] % CB for m in range(NC)]

    def multiply(src):
        lists_in(src).wait()
        q = src // 2
        h = src % 2
        for s in range(SECTIONS):
            first = q * SLOTS + s * SLOT
            filled = [msm[N + q, 0, BLOCKS + (s * R + row) * SLOT + t] for t in range(SLOT)]
            at = []
            for j in range(CB):
                entry = h * CB + j
                at.append(jnp.where(filled[0] == entry, first, jnp.where(filled[1] == entry, first + 1, none)))
            rows = [msm[src, 0, s * NA + a] for a in range(NA)]
            left = jnp.concatenate([abuf[src, pl.ds((s * NA + a) * BS, BS)] for a in range(NA)], axis=1)
            lhi = left.astype(jnp.bfloat16)
            llo = (left - lhi.astype(jnp.float32)).astype(jnp.bfloat16)
            highs, lows = [], []
            for m in range(NC):
                slot = jnp.where(wanted_j[m] == 0, at[0], at[1])
                places = [jnp.where(rows[a] == wanted_i[m], slot, none) for a in range(NA)]
                highs.append(jnp.concatenate([bhi[p] for p in places], axis=0))
                lows.append(jnp.concatenate([blo[p] for p in places], axis=0))
            rhi = jnp.concatenate(highs, axis=1)
            rlo = jnp.concatenate(lows, axis=1)
            total = jnp.dot(lhi, rhi, preferred_element_type=jnp.float32)
            total += jnp.dot(lhi, rlo, preferred_element_type=jnp.float32)
            total += jnp.dot(llo, rhi, preferred_element_type=jnp.float32)
            for m in range(NC):
                out_ref[0, 0, m] += total[:, m * BS:(m + 1) * BS]

    def mine(begin):
        multiply(2 * begin + y)

    def theirs(begin):
        for k in LATE[1:]:
            across_got(begin, k).wait_recv()
        multiply(2 * begin + 1 - y)

    near = min(2, L - 1)
    lax.fori_loop(1, near + 1, step, 0)
    each(0, near, lambda begin: lists_in(2 * begin + y).start())
    each(0, 0, lists_across)
    bbuf[none] = jnp.zeros((BS, BS), jnp.float32)
    for o in range(1, R):
        told(o).wait_recv()
    sides = pltpu.make_async_copy(mbuf.at[pl.ds(N, R)], msm.at[pl.ds(N, R)], lsem.at[3])
    sides.start()
    for o in range(1, R):
        give(o, (row - o + R) % R).wait_recv()
    lax.fori_loop(0, none + 1, split, 0)
    sides.wait()
    a_in.wait()
    c_in.wait()
    each(0, near, mine)
    each(0, 0, theirs)
    lax.fori_loop(near + 1, L, step, 0)
    each(near + 1, L - 1, lambda begin: lists_in(2 * begin + y).start())
    each(1, L - 1, lists_across)
    each(1, 1, theirs)
    each(near + 1, L - 1, mine)
    for d in range(2, near + 1):
        each(d, d, theirs)
    each(near + 1, L - 1, theirs)

    for begin in range(L):
        for k in LATE:
            across(begin, k).wait_send()
    across(z, EARLY).wait_send()

    def drain(d, carry):
        for ci in LINE:
            for up in (True, False):
                pl.when(line_sends(up, d))(lambda up=up, ci=ci: line(up, d, ci).wait_send())
        return carry

    lax.fori_loop(1, L, drain, 0)
    for o in range(1, R):
        give(o, row).wait_send()
        tell(o).wait_send()


def body(a_blocks, a_rows, b_blocks, send_list, c_partial, c_list):
    R = lax.axis_size("row")
    N = lax.axis_size("col")
    L = N // 2
    smem = pl.BlockSpec(memory_space=pltpu.SMEM)
    hbm = pl.BlockSpec(memory_space=pl.ANY)
    dma = pltpu.SemaphoreType.DMA
    return pl.pallas_call(
        functools.partial(kernel, R, N),
        out_shape=jax.ShapeDtypeStruct((1, 1, NC, BS, BS), jnp.float32),
        in_specs=[smem, smem, smem, hbm, hbm, hbm],
        out_specs=pl.BlockSpec(memory_space=pltpu.VMEM),
        scratch_shapes=[
            pltpu.VMEM((N, ROWS, BS), jnp.float32),
            pltpu.VMEM((SECTIONS, NB, BS, BS), jnp.float32),
            pltpu.VMEM((R, SLOTS, BS, BS), jnp.float32),
            pltpu.VMEM((R * SLOTS + 1, BS, BS), jnp.float32),
            pltpu.VMEM((R * SLOTS + 1, BS, BS), jnp.bfloat16),
            pltpu.VMEM((R * SLOTS + 1, BS, BS), jnp.bfloat16),
            pltpu.VMEM((1, 128), jnp.int32),
            pltpu.VMEM((N + R, 1, 128), jnp.int32),
            pltpu.SMEM((N + R, 1, 128), jnp.int32),
            dma((2, L, PIECES + 2)),
            dma((2, L, PIECES + 2)),
            dma((L, PIECES + 1)),
            dma((L, PIECES + 1)),
            dma((R,)),
            dma((R,)),
            dma((R,)),
            dma((R,)),
            dma((N,)),
            dma((4,)),
        ],
        compiler_params=pltpu.CompilerParams(
            collective_id=0, has_side_effects=True, vmem_limit_bytes=62 * 1024 * 1024
        ),
    )(
        a_rows, jnp.swapaxes(send_list, 3, 4), c_list,
        a_blocks.reshape(1, 1, ROWS, BS), b_blocks, c_partial,
    )


def solution(mesh):
    placed = (
        P("row", "col", None, None, None, None),
        P("row", "col", None, None),
        P("row", "col", None, None, None, None),
        P("row", "col", None, None, None),
        P("row", "col", None, None, None),
        P("row", "col", None),
    )
    return jax.shard_map(
        body,
        mesh=mesh,
        in_specs=placed,
        out_specs=P("row", "col", None, None, None),
        check_vma=False,
    )
```

```python
import functools

import jax
import jax.numpy as jnp
from jax import lax
from jax.experimental import pallas as pl
from jax.experimental.pallas import tpu as pltpu
from jax.sharding import PartitionSpec as P

BS = 128
SECTIONS = 2
NA = 2
SLOT = 2
NC = 4
NB = 4
CB = 2
BLOCKS = SECTIONS * NA
SLOTS = SECTIONS * SLOT
ROWS = BLOCKS * BS
CUTS = (0, 64, 128, 320, ROWS)
PIECES = len(CUTS) - 1
LISTS = PIECES
EARLY = (0, 1)
LATE = (LISTS,) + tuple(k for k in range(PIECES) if k not in EARLY)
OTHER = tuple(PIECES + 1 + k for k in range(len(EARLY)))
LINE = LATE + EARLY + OTHER
MESH = pl.DeviceIdType.MESH


def kernel(R, N, arows, slist, clist, a_ref, b_ref, cp_ref, out_ref,
           abuf, bsrc, stage, bbuf, bhi, blo, mtile, mbuf, msm,
           zsend, zrecv, ysend, yrecv, bsend, brecv, msend, mrecv, msem, lsem):
    L = N // 2
    row = lax.axis_index("row")
    col = lax.axis_index("col")
    z = col // 2
    y = col % 2
    pair = 2 * z + 1 - y

    barrier = pltpu.get_barrier_semaphore()
    pl.when(z + 1 < L)(lambda: pl.semaphore_signal(barrier, inc=1, device_id=(row, col + 2), device_id_type=MESH))
    pl.when(z >= 1)(lambda: pl.semaphore_signal(barrier, inc=1, device_id=(row, col - 2), device_id_type=MESH))
    pl.semaphore_signal(barrier, inc=1, device_id=(row, pair), device_id_type=MESH)
    for o in range(1, R):
        pl.semaphore_signal(barrier, inc=1, device_id=((row + o) % R, col), device_id_type=MESH)

    b_in = pltpu.make_async_copy(b_ref.at[0, 0], bsrc, lsem.at[0])
    a_in = pltpu.make_async_copy(a_ref.at[0, 0], abuf.at[col], lsem.at[1])
    c_in = pltpu.make_async_copy(cp_ref.at[0, 0], out_ref.at[0, 0], lsem.at[2])
    b_in.start()
    a_in.start()
    c_in.start()

    lane = lax.broadcasted_iota(jnp.int32, (1, 128), 1)
    tile = jnp.zeros((1, 128), jnp.int32)
    for s in range(SECTIONS):
        for a in range(NA):
            tile = jnp.where(lane == s * NA + a, arows[0, 0, s, a], tile)
        for r in range(R):
            for t in range(SLOT):
                tile = jnp.where(lane == BLOCKS + (s * R + r) * SLOT + t, slist[0, 0, s, t, r], tile)
    mtile[...] = tile
    mbuf[col] = tile
    mbuf[N + row] = tile

    edge = jnp.where(z + 1 < L, 1, 0) + jnp.where(z >= 1, 1, 0)
    pl.semaphore_wait(barrier, R + edge)

    def own(k):
        return mtile if k == LISTS else a_ref.at[0, 0, pl.ds(CUTS[k], CUTS[k + 1] - CUTS[k])]

    def held(src, k):
        return mbuf.at[src] if k == LISTS else abuf.at[src, pl.ds(CUTS[k], CUTS[k + 1] - CUTS[k])]

    def line_piece(begin, ci):
        return (2 * begin + 1 - y, EARLY[ci - PIECES - 1]) if ci in OTHER else (2 * begin + y, ci)

    def line(up, d, ci, first=False):
        src, k = line_piece(z - (d - 1) if up else z + (d - 1), ci)
        way = 0 if up else 1
        return pltpu.make_async_remote_copy(
            src_ref=own(k) if first and ci not in OTHER else held(src, k),
            dst_ref=held(src, k),
            send_sem=zsend.at[way, d - 1, ci],
            recv_sem=zrecv.at[way, d - 1, ci],
            device_id=(row, col + 2 if up else col - 2),
            device_id_type=MESH,
        )

    def line_sends(up, d, ci):
        begin = z - (d - 1) if up else z + (d - 1)
        follows = z + 1 < L if up else z >= 1
        if ci in OTHER:
            return jnp.logical_and(follows, begin == (0 if up else L - 1))
        return jnp.logical_and(follows, begin >= 0 if up else begin < L)

    def line_gets(up, d, ci):
        begin = z - d if up else z + d
        if ci in OTHER:
            return begin == (0 if up else L - 1)
        return begin >= 0 if up else begin < L

    def inner(begin):
        return jnp.logical_and(begin > 0, begin < L - 1)

    def line_got(up, d, ci):
        src, k = line_piece(z - d if up else z + d, ci)
        way = 0 if up else 1
        return pltpu.make_async_remote_copy(
            src_ref=held(src, k), dst_ref=held(src, k),
            send_sem=zsend.at[way, d - 1, ci], recv_sem=zrecv.at[way, d - 1, ci],
            device_id=(row, pair), device_id_type=MESH)

    def across(begin, k, first=False):
        src = 2 * begin + y
        return pltpu.make_async_remote_copy(
            src_ref=own(k) if first else held(src, k), dst_ref=held(src, k),
            send_sem=ysend.at[begin, k], recv_sem=yrecv.at[begin, k],
            device_id=(row, pair), device_id_type=MESH)

    def across_got(begin, k):
        src = 2 * begin + 1 - y
        return pltpu.make_async_remote_copy(
            src_ref=held(src, k), dst_ref=held(src, k),
            send_sem=ysend.at[begin, k], recv_sem=yrecv.at[begin, k],
            device_id=(row, pair), device_id_type=MESH)

    for k, m in zip((LISTS,) + EARLY + LATE[1:], LATE + EARLY):
        across(z, k, True).start()
        for up in (True, False):
            pl.when(line_sends(up, 1, m))(lambda up=up, m=m: line(up, 1, m, True).start())

    def tell(o):
        return pltpu.make_async_remote_copy(
            src_ref=mtile, dst_ref=mbuf.at[N + row], send_sem=msend.at[o], recv_sem=mrecv.at[o],
            device_id=((row + o) % R, col), device_id_type=MESH)

    def told(o):
        return pltpu.make_async_remote_copy(
            src_ref=mtile, dst_ref=mbuf.at[N + (row - o + R) % R], send_sem=msend.at[o], recv_sem=mrecv.at[o],
            device_id=(row, pair), device_id_type=MESH)

    for o in range(1, R):
        tell(o).start()

    b_in.wait()

    def give(o, q):
        return pltpu.make_async_remote_copy(
            src_ref=stage.at[o], dst_ref=bbuf.at[pl.ds(q * SLOTS, SLOTS)],
            send_sem=bsend.at[o], recv_sem=brecv.at[o],
            device_id=((row + o) % R, col), device_id_type=MESH)

    for o in sorted(range(R), key=lambda o: (o == 0, abs(o - R // 2))):
        to = (row + o) % R
        for s in range(SECTIONS):
            for t in range(SLOT):
                entry = jnp.maximum(slist[0, 0, s, t, to], 0)
                if o:
                    stage[o, s * SLOT + t] = bsrc[s, entry]
                else:
                    bbuf[row * SLOTS + s * SLOT + t] = bsrc[s, entry]
        if o:
            give(o, row).start()

    for k, ci in zip(EARLY, OTHER):
        across_got(z, k).wait_recv()
        for up in (True, False):
            pl.when(line_sends(up, 1, ci))(lambda up=up, ci=ci: line(up, 1, ci).start())

    def step(d, carry):
        for ci in LINE:
            for up in (True, False):
                @pl.when(line_gets(up, d, ci))
                def _():
                    begin = z - d if up else z + d
                    line_got(up, d, ci).wait_recv()
                    pl.when(line_sends(up, d + 1, ci))(lambda: line(up, d + 1, ci).start())
                    if ci in LATE:
                        across(begin, ci).start()
                    elif ci in EARLY:
                        pl.when(inner(begin))(lambda: across(begin, ci).start())
        return carry

    none = R * SLOTS

    def split(at, carry):
        block = bbuf[at]
        high = block.astype(jnp.bfloat16)
        bhi[at] = high
        blo[at] = (block - high.astype(jnp.float32)).astype(jnp.bfloat16)
        return carry

    def lists_in(src):
        return pltpu.make_async_copy(mbuf.at[src], msm.at[src], msem.at[src])

    def each(least, most, do):
        def one(begin, carry):
            away = jnp.maximum(begin - z, z - begin)
            pl.when(jnp.logical_and(away >= least, away <= most))(lambda: do(begin))
            return carry
        lax.fori_loop(0, L, one, 0)

    def lists_across(begin):
        across_got(begin, LISTS).wait_recv()
        lists_in(2 * begin + 1 - y).start()

    wanted_i = [clist[0, 0, m] // CB for m in range(NC)]
    wanted_j = [clist[0, 0, m] % CB for m in range(NC)]

    def multiply(src):
        lists_in(src).wait()
        q = src // 2
        h = src % 2
        for s in range(SECTIONS):
            first = q * SLOTS + s * SLOT
            filled = [msm[N + q, 0, BLOCKS + (s * R + row) * SLOT + t] for t in range(SLOT)]
            at = []
            for j in range(CB):
                entry = h * CB + j
                at.append(jnp.where(filled[0] == entry, first, jnp.where(filled[1] == entry, first + 1, none)))
            rows = [msm[src, 0, s * NA + a] for a in range(NA)]
            left = jnp.concatenate([abuf[src, pl.ds((s * NA + a) * BS, BS)] for a in range(NA)], axis=1)
            lhi = left.astype(jnp.bfloat16)
            llo = (left - lhi.astype(jnp.float32)).astype(jnp.bfloat16)
            highs, lows = [], []
            for m in range(NC):
                slot = jnp.where(wanted_j[m] == 0, at[0], at[1])
                places = [jnp.where(rows[a] == wanted_i[m], slot, none) for a in range(NA)]
                highs.append(jnp.concatenate([bhi[p] for p in places], axis=0))
                lows.append(jnp.concatenate([blo[p] for p in places], axis=0))
            rhi = jnp.concatenate(highs, axis=1)
            rlo = jnp.concatenate(lows, axis=1)
            total = jnp.dot(lhi, rhi, preferred_element_type=jnp.float32)
            total += jnp.dot(lhi, rlo, preferred_element_type=jnp.float32)
            total += jnp.dot(llo, rhi, preferred_element_type=jnp.float32)
            for m in range(NC):
                out_ref[0, 0, m] += total[:, m * BS:(m + 1) * BS]

    def mine(begin):
        multiply(2 * begin + y)

    def theirs(begin):
        for k in LATE[1:]:
            across_got(begin, k).wait_recv()
        for k in EARLY:
            pl.when(jnp.logical_and(inner(begin), begin != z))(lambda k=k: across_got(begin, k).wait_recv())
        multiply(2 * begin + 1 - y)

    near = min(2, L - 1)
    lax.fori_loop(1, near + 1, step, 0)
    each(0, near, lambda begin: lists_in(2 * begin + y).start())
    each(0, 0, lists_across)
    bbuf[none] = jnp.zeros((BS, BS), jnp.float32)
    for o in range(1, R):
        told(o).wait_recv()
    sides = pltpu.make_async_copy(mbuf.at[pl.ds(N, R)], msm.at[pl.ds(N, R)], lsem.at[3])
    sides.start()
    for o in range(1, R):
        give(o, (row - o + R) % R).wait_recv()
    lax.fori_loop(0, none + 1, split, 0)
    sides.wait()
    a_in.wait()
    c_in.wait()
    each(0, near, mine)
    each(0, 0, theirs)
    lax.fori_loop(near + 1, L, step, 0)
    each(near + 1, L - 1, lambda begin: lists_in(2 * begin + y).start())
    each(1, L - 1, lists_across)
    each(1, 1, theirs)
    each(near + 1, L - 1, mine)
    for d in range(2, near + 1):
        each(d, d, theirs)
    each(near + 1, L - 1, theirs)

    for begin in range(L):
        begin = jnp.int32(begin)
        for k in LATE:
            across(begin, k).wait_send()
        for k in EARLY:
            pl.when(jnp.logical_or(inner(begin), begin == z))(lambda k=k: across(begin, k).wait_send())

    def drain(d, carry):
        for ci in LINE:
            for up in (True, False):
                pl.when(line_sends(up, d, ci))(lambda up=up, ci=ci: line(up, d, ci).wait_send())
        return carry

    lax.fori_loop(1, L, drain, 0)
    for o in range(1, R):
        give(o, row).wait_send()
        tell(o).wait_send()


def body(a_blocks, a_rows, b_blocks, send_list, c_partial, c_list):
    R = lax.axis_size("row")
    N = lax.axis_size("col")
    L = N // 2
    smem = pl.BlockSpec(memory_space=pltpu.SMEM)
    hbm = pl.BlockSpec(memory_space=pl.ANY)
    dma = pltpu.SemaphoreType.DMA
    return pl.pallas_call(
        functools.partial(kernel, R, N),
        out_shape=jax.ShapeDtypeStruct((1, 1, NC, BS, BS), jnp.float32),
        in_specs=[smem, smem, smem, hbm, hbm, hbm],
        out_specs=pl.BlockSpec(memory_space=pltpu.VMEM),
        scratch_shapes=[
            pltpu.VMEM((N, ROWS, BS), jnp.float32),
            pltpu.VMEM((SECTIONS, NB, BS, BS), jnp.float32),
            pltpu.VMEM((R, SLOTS, BS, BS), jnp.float32),
            pltpu.VMEM((R * SLOTS + 1, BS, BS), jnp.float32),
            pltpu.VMEM((R * SLOTS + 1, BS, BS), jnp.bfloat16),
            pltpu.VMEM((R * SLOTS + 1, BS, BS), jnp.bfloat16),
            pltpu.VMEM((1, 128), jnp.int32),
            pltpu.VMEM((N + R, 1, 128), jnp.int32),
            pltpu.SMEM((N + R, 1, 128), jnp.int32),
            dma((2, L, PIECES + 1 + len(EARLY))),
            dma((2, L, PIECES + 1 + len(EARLY))),
            dma((L, PIECES + 1)),
            dma((L, PIECES + 1)),
            dma((R,)),
            dma((R,)),
            dma((R,)),
            dma((R,)),
            dma((N,)),
            dma((4,)),
        ],
        compiler_params=pltpu.CompilerParams(
            collective_id=0, has_side_effects=True, vmem_limit_bytes=62 * 1024 * 1024
        ),
    )(
        a_rows, jnp.swapaxes(send_list, 3, 4), c_list,
        a_blocks.reshape(1, 1, ROWS, BS), b_blocks, c_partial,
    )


def solution(mesh):
    placed = (
        P("row", "col", None, None, None, None),
        P("row", "col", None, None),
        P("row", "col", None, None, None, None),
        P("row", "col", None, None, None),
        P("row", "col", None, None, None),
        P("row", "col", None),
    )
    return jax.shard_map(
        body,
        mesh=mesh,
        in_specs=placed,
        out_specs=P("row", "col", None, None, None),
        check_vma=False,
    )
```

```python
import functools

import jax
import jax.numpy as jnp
from jax import lax
from jax.experimental import pallas as pl
from jax.experimental.pallas import tpu as pltpu
from jax.sharding import PartitionSpec as P

BS = 128
SECTIONS = 2
NA = 2
SLOT = 2
NC = 4
NB = 4
CB = 2
BLOCKS = SECTIONS * NA
SLOTS = SECTIONS * SLOT
ROWS = BLOCKS * BS
CUTS = (0, 144, 328, ROWS)
PIECES = len(CUTS) - 1
LISTS = PIECES
EARLY = (0,)
LATE = (LISTS,) + tuple(k for k in range(PIECES) if k not in EARLY)
OTHER = tuple(PIECES + 1 + k for k in range(len(EARLY)))
LINE = LATE + EARLY + OTHER
MESH = pl.DeviceIdType.MESH


def kernel(R, N, arows, slist, clist, a_ref, b_ref, cp_ref, out_ref,
           abuf, bsrc, stage, bbuf, bhi, blo, mtile, mbuf, msm,
           zsend, zrecv, ysend, yrecv, bsend, brecv, msend, mrecv, msem, lsem):
    L = N // 2
    row = lax.axis_index("row")
    col = lax.axis_index("col")
    z = col // 2
    y = col % 2
    pair = 2 * z + 1 - y

    barrier = pltpu.get_barrier_semaphore()
    pl.when(z + 1 < L)(lambda: pl.semaphore_signal(barrier, inc=1, device_id=(row, col + 2), device_id_type=MESH))
    pl.when(z >= 1)(lambda: pl.semaphore_signal(barrier, inc=1, device_id=(row, col - 2), device_id_type=MESH))
    pl.semaphore_signal(barrier, inc=1, device_id=(row, pair), device_id_type=MESH)
    for o in range(1, R):
        pl.semaphore_signal(barrier, inc=1, device_id=((row + o) % R, col), device_id_type=MESH)

    b_in = pltpu.make_async_copy(b_ref.at[0, 0], bsrc, lsem.at[0])
    a_in = pltpu.make_async_copy(a_ref.at[0, 0], abuf.at[col], lsem.at[1])
    c_in = pltpu.make_async_copy(cp_ref.at[0, 0], out_ref.at[0, 0], lsem.at[2])
    b_in.start()
    a_in.start()
    c_in.start()

    lane = lax.broadcasted_iota(jnp.int32, (1, 128), 1)
    tile = jnp.zeros((1, 128), jnp.int32)
    for s in range(SECTIONS):
        for a in range(NA):
            tile = jnp.where(lane == s * NA + a, arows[0, 0, s, a], tile)
        for r in range(R):
            for t in range(SLOT):
                tile = jnp.where(lane == BLOCKS + (s * R + r) * SLOT + t, slist[0, 0, s, t, r], tile)
    mtile[...] = tile
    mbuf[col] = tile
    mbuf[N + row] = tile

    a_in.wait()
    edge = jnp.where(z + 1 < L, 1, 0) + jnp.where(z >= 1, 1, 0)
    pl.semaphore_wait(barrier, R + edge)

    def own(k):
        return held(col, k)

    def held(src, k):
        return mbuf.at[src] if k == LISTS else abuf.at[src, pl.ds(CUTS[k], CUTS[k + 1] - CUTS[k])]

    def line_piece(begin, ci):
        return (2 * begin + 1 - y, EARLY[ci - PIECES - 1]) if ci in OTHER else (2 * begin + y, ci)

    def line(up, d, ci, first=False):
        src, k = line_piece(z - (d - 1) if up else z + (d - 1), ci)
        way = 0 if up else 1
        return pltpu.make_async_remote_copy(
            src_ref=own(k) if first and ci not in OTHER else held(src, k),
            dst_ref=held(src, k),
            send_sem=zsend.at[way, d - 1, ci],
            recv_sem=zrecv.at[way, d - 1, ci],
            device_id=(row, col + 2 if up else col - 2),
            device_id_type=MESH,
        )

    def line_sends(up, d, ci):
        begin = z - (d - 1) if up else z + (d - 1)
        follows = z + 1 < L if up else z >= 1
        if ci in OTHER:
            return jnp.logical_and(follows, begin == (0 if up else L - 1))
        return jnp.logical_and(follows, begin >= 0 if up else begin < L)

    def line_gets(up, d, ci):
        begin = z - d if up else z + d
        if ci in OTHER:
            return begin == (0 if up else L - 1)
        return begin >= 0 if up else begin < L

    def inner(begin):
        return jnp.logical_and(begin > 0, begin < L - 1)

    def line_got(up, d, ci):
        src, k = line_piece(z - d if up else z + d, ci)
        way = 0 if up else 1
        return pltpu.make_async_remote_copy(
            src_ref=held(src, k), dst_ref=held(src, k),
            send_sem=zsend.at[way, d - 1, ci], recv_sem=zrecv.at[way, d - 1, ci],
            device_id=(row, pair), device_id_type=MESH)

    def across(begin, k, first=False):
        src = 2 * begin + y
        return pltpu.make_async_remote_copy(
            src_ref=own(k) if first else held(src, k), dst_ref=held(src, k),
            send_sem=ysend.at[begin, k], recv_sem=yrecv.at[begin, k],
            device_id=(row, pair), device_id_type=MESH)

    def across_got(begin, k):
        src = 2 * begin + 1 - y
        return pltpu.make_async_remote_copy(
            src_ref=held(src, k), dst_ref=held(src, k),
            send_sem=ysend.at[begin, k], recv_sem=yrecv.at[begin, k],
            device_id=(row, pair), device_id_type=MESH)

    for k, m in zip((LISTS,) + EARLY + LATE[1:], LATE + EARLY):
        across(z, k, True).start()
        for up in (True, False):
            pl.when(line_sends(up, 1, m))(lambda up=up, m=m: line(up, 1, m, True).start())

    def tell(o):
        return pltpu.make_async_remote_copy(
            src_ref=mtile, dst_ref=mbuf.at[N + row], send_sem=msend.at[o], recv_sem=mrecv.at[o],
            device_id=((row + o) % R, col), device_id_type=MESH)

    def told(o):
        return pltpu.make_async_remote_copy(
            src_ref=mtile, dst_ref=mbuf.at[N + (row - o + R) % R], send_sem=msend.at[o], recv_sem=mrecv.at[o],
            device_id=(row, pair), device_id_type=MESH)

    for o in range(1, R):
        tell(o).start()

    b_in.wait()

    def give(o, q):
        return pltpu.make_async_remote_copy(
            src_ref=stage.at[o], dst_ref=bbuf.at[pl.ds(q * SLOTS, SLOTS)],
            send_sem=bsend.at[o], recv_sem=brecv.at[o],
            device_id=((row + o) % R, col), device_id_type=MESH)

    for o in sorted(range(R), key=lambda o: (o == 0, abs(o - R // 2))):
        to = (row + o) % R
        for s in range(SECTIONS):
            for t in range(SLOT):
                entry = jnp.maximum(slist[0, 0, s, t, to], 0)
                if o:
                    stage[o, s * SLOT + t] = bsrc[s, entry]
                else:
                    bbuf[row * SLOTS + s * SLOT + t] = bsrc[s, entry]
        if o:
            give(o, row).start()

    for k, ci in zip(EARLY, OTHER):
        across_got(z, k).wait_recv()
        for up in (True, False):
            pl.when(line_sends(up, 1, ci))(lambda up=up, ci=ci: line(up, 1, ci).start())

    def step(d, carry):
        for ci in LINE:
            for up in (True, False):
                @pl.when(line_gets(up, d, ci))
                def _():
                    begin = z - d if up else z + d
                    line_got(up, d, ci).wait_recv()
                    pl.when(line_sends(up, d + 1, ci))(lambda: line(up, d + 1, ci).start())
                    if ci in LATE:
                        across(begin, ci).start()
                    elif ci in EARLY:
                        pl.when(inner(begin))(lambda: across(begin, ci).start())
        return carry

    none = R * SLOTS

    def split(at, carry):
        block = bbuf[at]
        high = block.astype(jnp.bfloat16)
        bhi[at] = high
        blo[at] = (block - high.astype(jnp.float32)).astype(jnp.bfloat16)
        return carry

    def lists_in(src):
        return pltpu.make_async_copy(mbuf.at[src], msm.at[src], msem.at[src])

    def each(least, most, do):
        def one(begin, carry):
            away = jnp.maximum(begin - z, z - begin)
            pl.when(jnp.logical_and(away >= least, away <= most))(lambda: do(begin))
            return carry
        lax.fori_loop(0, L, one, 0)

    def lists_across(begin):
        across_got(begin, LISTS).wait_recv()
        lists_in(2 * begin + 1 - y).start()

    wanted_i = [clist[0, 0, m] // CB for m in range(NC)]
    wanted_j = [clist[0, 0, m] % CB for m in range(NC)]

    def multiply(src):
        lists_in(src).wait()
        q = src // 2
        h = src % 2
        for s in range(SECTIONS):
            first = q * SLOTS + s * SLOT
            filled = [msm[N + q, 0, BLOCKS + (s * R + row) * SLOT + t] for t in range(SLOT)]
            at = []
            for j in range(CB):
                entry = h * CB + j
                at.append(jnp.where(filled[0] == entry, first, jnp.where(filled[1] == entry, first + 1, none)))
            rows = [msm[src, 0, s * NA + a] for a in range(NA)]
            left = jnp.concatenate([abuf[src, pl.ds((s * NA + a) * BS, BS)] for a in range(NA)], axis=1)
            lhi = left.astype(jnp.bfloat16)
            llo = (left - lhi.astype(jnp.float32)).astype(jnp.bfloat16)
            highs, lows = [], []
            for m in range(NC):
                slot = jnp.where(wanted_j[m] == 0, at[0], at[1])
                places = [jnp.where(rows[a] == wanted_i[m], slot, none) for a in range(NA)]
                highs.append(jnp.concatenate([bhi[p] for p in places], axis=0))
                lows.append(jnp.concatenate([blo[p] for p in places], axis=0))
            rhi = jnp.concatenate(highs, axis=1)
            rlo = jnp.concatenate(lows, axis=1)
            total = jnp.dot(lhi, rhi, preferred_element_type=jnp.float32)
            total += jnp.dot(lhi, rlo, preferred_element_type=jnp.float32)
            total += jnp.dot(llo, rhi, preferred_element_type=jnp.float32)
            for m in range(NC):
                out_ref[0, 0, m] += total[:, m * BS:(m + 1) * BS]

    def mine(begin):
        multiply(2 * begin + y)

    def theirs(begin):
        for k in LATE[1:]:
            across_got(begin, k).wait_recv()
        for k in EARLY:
            pl.when(jnp.logical_and(inner(begin), begin != z))(lambda k=k: across_got(begin, k).wait_recv())
        multiply(2 * begin + 1 - y)

    near = min(2, L - 1)
    lax.fori_loop(1, near + 1, step, 0)
    each(0, near, lambda begin: lists_in(2 * begin + y).start())
    each(0, 0, lists_across)
    bbuf[none] = jnp.zeros((BS, BS), jnp.float32)
    for o in range(1, R):
        told(o).wait_recv()
    sides = pltpu.make_async_copy(mbuf.at[pl.ds(N, R)], msm.at[pl.ds(N, R)], lsem.at[3])
    sides.start()
    for o in range(1, R):
        give(o, (row - o + R) % R).wait_recv()
    lax.fori_loop(0, none + 1, split, 0)
    sides.wait()
    c_in.wait()
    each(0, near, mine)
    each(0, 0, theirs)
    lax.fori_loop(near + 1, L, step, 0)
    each(near + 1, L - 1, lambda begin: lists_in(2 * begin + y).start())
    each(1, L - 1, lists_across)
    each(1, 1, theirs)
    each(near + 1, L - 1, mine)
    for d in range(2, near + 1):
        each(d, d, theirs)
    each(near + 1, L - 1, theirs)

    for begin in range(L):
        begin = jnp.int32(begin)
        for k in LATE:
            across(begin, k).wait_send()
        for k in EARLY:
            pl.when(jnp.logical_or(inner(begin), begin == z))(lambda k=k: across(begin, k).wait_send())

    def drain(d, carry):
        for ci in LINE:
            for up in (True, False):
                pl.when(line_sends(up, d, ci))(lambda up=up, ci=ci: line(up, d, ci).wait_send())
        return carry

    lax.fori_loop(1, L, drain, 0)
    for o in range(1, R):
        give(o, row).wait_send()
        tell(o).wait_send()


def body(a_blocks, a_rows, b_blocks, send_list, c_partial, c_list):
    R = lax.axis_size("row")
    N = lax.axis_size("col")
    L = N // 2
    smem = pl.BlockSpec(memory_space=pltpu.SMEM)
    hbm = pl.BlockSpec(memory_space=pl.ANY)
    dma = pltpu.SemaphoreType.DMA
    return pl.pallas_call(
        functools.partial(kernel, R, N),
        out_shape=jax.ShapeDtypeStruct((1, 1, NC, BS, BS), jnp.float32),
        in_specs=[smem, smem, smem, hbm, hbm, hbm],
        out_specs=pl.BlockSpec(memory_space=pltpu.VMEM),
        scratch_shapes=[
            pltpu.VMEM((N, ROWS, BS), jnp.float32),
            pltpu.VMEM((SECTIONS, NB, BS, BS), jnp.float32),
            pltpu.VMEM((R, SLOTS, BS, BS), jnp.float32),
            pltpu.VMEM((R * SLOTS + 1, BS, BS), jnp.float32),
            pltpu.VMEM((R * SLOTS + 1, BS, BS), jnp.bfloat16),
            pltpu.VMEM((R * SLOTS + 1, BS, BS), jnp.bfloat16),
            pltpu.VMEM((1, 128), jnp.int32),
            pltpu.VMEM((N + R, 1, 128), jnp.int32),
            pltpu.SMEM((N + R, 1, 128), jnp.int32),
            dma((2, L, PIECES + 1 + len(EARLY))),
            dma((2, L, PIECES + 1 + len(EARLY))),
            dma((L, PIECES + 1)),
            dma((L, PIECES + 1)),
            dma((R,)),
            dma((R,)),
            dma((R,)),
            dma((R,)),
            dma((N,)),
            dma((4,)),
        ],
        compiler_params=pltpu.CompilerParams(
            collective_id=0, has_side_effects=True, vmem_limit_bytes=62 * 1024 * 1024
        ),
    )(
        a_rows, jnp.swapaxes(send_list, 3, 4), c_list,
        a_blocks.reshape(1, 1, ROWS, BS), b_blocks, c_partial,
    )


def solution(mesh):
    placed = (
        P("row", "col", None, None, None, None),
        P("row", "col", None, None),
        P("row", "col", None, None, None, None),
        P("row", "col", None, None, None),
        P("row", "col", None, None, None),
        P("row", "col", None),
    )
    return jax.shard_map(
        body,
        mesh=mesh,
        in_specs=placed,
        out_specs=P("row", "col", None, None, None),
        check_vma=False,
    )
```
